256 devices in a mesh: slab: 8 (over z_lo, y), vocab: 32 (over x, z_hi, core).
Axes of the slice: x: 4, y: 4, z: 8 (z_hi: 4, z_lo: 2; z = z_hi * 2 + z_lo), core: 2. Of those that a mesh axis runs over, the one named last changes fastest.
Arguments:
- teacher_ids: int32 [1024], replicated, may hold values from 0 to 152063
- slab_embed: bfloat16 [1024, 8192], P('slab', 'vocab'), may hold values from -2 to 2
- projection: bfloat16 [8192, 3072], P('vocab', 'slab'), may hold values from -0.0625 to 0.0625
- learner_vector_table: bfloat16 [65536, 3072], P('vocab', 'slab'), may hold values from -6 to 6
- teacher_dual: float32 [152064], replicated, may hold values from 1.055 to 1.08
- student_dual: float32 [65536], P('vocab'), may hold values from -0.05 to 0.05
Outputs:
- grad_projection: bfloat16 [8192, 3072], P('vocab', 'slab')
- grad_slab: bfloat16 [1024, 8192], P('slab', 'vocab')
- grad_student: bfloat16 [65536, 3072], P('vocab', 'slab')
The draws below stay inside these ranges and needn't reach their ends.
All inputs are finite; a program needn't handle non-finite values.
Results may differ from the reference program's by a relative error of at most 0.0056.
Values may be sent and summed in bfloat16 or wider, within the bound.
A program may use at most 64 MiB of HBM per device.

```python
import math
import jax
import jax.numpy as jnp
import numpy as np
from jax import lax

DT = 8192
DS = 3072
TVOCAB = 152064
VOC_DEV = 2048
ROWS = 1024
VOCAB = 65536


def draw_slab_embed(key, part):
    key = jax.random.fold_in(key, 7)
    values = jnp.clip(0.4 * jax.random.normal(key, (ROWS, DT), jnp.float32), -2.0, 2.0)
    return values.astype(jnp.bfloat16)


def with_ends(values, key, low, largest):
    extent = values.shape
    spot = [jax.random.randint(jax.random.fold_in(key, axis), (), 0, extent[axis]) for axis in range(len(extent))]
    values = values.at[tuple(spot)].set(low)
    longest = extent.index(max(extent))
    spot[longest] = (spot[longest] + 1) % extent[longest]
    return values.at[tuple(spot)].set(largest)


def block_scale(rng, extent, pieces, least, largest):
    loudness, own = 1.0, jax.random.fold_in(rng, 6)
    for dim, parts in pieces:
        heights = jnp.exp(jax.random.uniform(jax.random.fold_in(own, dim), (parts,), jnp.float32, least / len(pieces), largest / len(pieces)))
        loudness = loudness * jnp.repeat(heights, extent[dim] // parts).reshape([-1 if axis == dim else 1 for axis in range(len(extent))])
    return loudness


def ranked_wide(key, extent, count, skew):
    loads = [min(1 << octave, count + 1 - (1 << octave)) * (1 << 20) // math.isqrt((1 << octave) ** skew) + 1 for octave in range((count + 1).bit_length()) if 1 << octave <= count]
    scale = 1 + sum(loads) // (1 << 30)
    listing = np.cumsum(np.array([max(1, weight // scale) for weight in loads]))
    pick = jax.random.randint(jax.random.fold_in(key, 1), extent, 0, int(listing[len(loads) - 1]))
    start = jnp.left_shift(1, jnp.searchsorted(jnp.asarray(listing, jnp.int32), pick, side="right").astype(jnp.int32))
    grade = start - 1 + jax.random.randint(jax.random.fold_in(key, 4), extent, 0, 1 << 30) % jnp.minimum(start, count + 1 - start)
    return jax.random.permutation(jax.random.fold_in(key, 2), count)[grade].astype(jnp.int32)


def normal_values(stream_key, dims, scale, reach, cuts=(), dtype=jnp.bfloat16):
    entries = scale * jax.random.normal(stream_key, dims, jnp.float32)
    if cuts:
        entries = entries * block_scale(stream_key, dims, cuts, -0.22, 0.18)
    return jnp.clip(entries, -reach, reach).astype(dtype)


def setup_inputs(seed: int = 0) -> dict:
    key_list = jax.random.split(jax.random.key(seed), 7)
    teacher_ids = with_ends(ranked_wide(key_list[0], (ROWS,), TVOCAB, 2), jax.random.fold_in(key_list[0], 3), 0, TVOCAB - 1).astype(jnp.int32)
    slab_embed = draw_slab_embed(jax.random.fold_in(key_list[6], 71), 0)
    projection = normal_values(key_list[2], (DT, DS), DT ** -0.5, 0.0625, ((0, 32), (1, 8)))
    learner_vector_table = normal_values(key_list[3], (VOCAB, DS), 1.0, 6.0, ((0, 32), (1, 8)))
    teacher_dual = jnp.clip(jax.random.uniform(key_list[4], (TVOCAB,), jnp.float32, 1.055, 1.08), 1.055, 1.08)
    student_dual = jnp.clip(jax.random.uniform(key_list[5], (VOCAB,), jnp.float32, -0.05, 0.05) * block_scale(key_list[5], (VOCAB,), ((0, 32),), -0.4, 0.0), -0.05, 0.05)
    return dict(teacher_ids=teacher_ids, slab_embed=slab_embed, projection=projection, learner_vector_table=learner_vector_table, teacher_dual=teacher_dual, student_dual=student_dual)


smoothing_strength = 0.04

def reference(teacher_ids, slab_embed, projection, learner_vector_table, teacher_dual, student_dual):
    source_dual_vector = teacher_dual[teacher_ids]
    projected = jnp.dot(slab_embed, projection, preferred_element_type=jnp.float32).astype(jnp.bfloat16)
    projected_f = projected.astype(jnp.float32)
    proj_square = lax.optimization_barrier(jnp.sum(projected_f * projected_f, axis=1))
    blocks = VOCAB // VOC_DEV
    embed_blocks = learner_vector_table.reshape(blocks, VOC_DEV, DS)
    dual_blocks = student_dual.reshape(blocks, VOC_DEV)

    def one_block(carried, pair):
        embed_part, dual_variable_slice = pair
        embed_f = embed_part.astype(jnp.float32)
        inner = jnp.dot(projected, embed_part.T, preferred_element_type=jnp.float32)
        ground_distance_matrix = (proj_square[:, None] + lax.optimization_barrier(jnp.sum(embed_f * embed_f, axis=1))[None, :] - 2.0 * inner) / DS
        exponential_affinity_matrix = jnp.exp((source_dual_vector[:, None] + dual_variable_slice[None, :] - ground_distance_matrix) / smoothing_strength).astype(jnp.bfloat16)
        kernel_f = exponential_affinity_matrix.astype(jnp.float32)
        row_part = lax.optimization_barrier(jnp.sum(kernel_f, axis=1))[:, None] * projected_f - jnp.dot(exponential_affinity_matrix, embed_part, preferred_element_type=jnp.float32)
        col_mass = lax.optimization_barrier(jnp.sum(kernel_f, axis=0))
        student_part = (col_mass[:, None] * embed_f - jnp.dot(exponential_affinity_matrix.T, projected, preferred_element_type=jnp.float32)) / ROWS
        return (carried + row_part, student_part.astype(jnp.bfloat16))
    row_term, student_grads = lax.scan(one_block, jnp.zeros((ROWS, DS), jnp.float32), (embed_blocks, dual_blocks))
    row_grad = (row_term / VOCAB).astype(jnp.bfloat16)
    grad_student = student_grads.reshape(VOCAB, DS)
    grad_slab = jnp.dot(row_grad, projection.T, preferred_element_type=jnp.float32).astype(jnp.bfloat16)
    grad_projection = (jnp.dot(slab_embed.T, row_grad, preferred_element_type=jnp.float32) / jnp.sqrt(jnp.float32(ROWS))).astype(jnp.bfloat16)
    return (grad_projection, grad_slab, grad_student)
```

```python
import jax
import jax.numpy as jnp
from jax import lax
from jax.experimental import pallas as pl
from jax.experimental.pallas import tpu as pltpu
from jax.sharding import PartitionSpec as P

DS = 3072
ROWS = 1024
VOCAB = 65536
STRENGTH = 0.04
FB = 384
DUAL_ROWS = 1280
NSEM = 112
F32, BF16 = jnp.float32, jnp.bfloat16
MESH = pl.DeviceIdType.MESH


def dot_last(a, b):
    return lax.dot_general(a, b, (((1,), (1,)), ((), ())), preferred_element_type=F32)


def dot_first(a, b):
    return lax.dot_general(a, b, (((0,), (0,)), ((), ())), preferred_element_type=F32)


def dot(a, b):
    return jnp.dot(a, b, preferred_element_type=F32)


def al(value, size):
    return pl.multiple_of(value, size)


def kernel(
    ids_ref, slab_ref, proj_ref, table_ref, dual_ref, sdual_ref,
    gp_ref, gs_ref, gst_ref,
    xg, sx, sdb, crecv, csend, acc, xsend, xrecv, zsend, zrecv, pown, pbuf,
    rd, qrow, kb, kt, rbuf, ra1, rb1, ra2, rb2, ra2r, rb2r, rz, rzr,
    rgown, rg, stsend, strecv, stown, gown, fsend, frecv,
    ssem, rsem, lsem,
):
    s = lax.axis_index("slab")
    v = lax.axis_index("vocab")
    zlo, y = lax.div(s, 4), lax.rem(s, 4)
    core, zhi, x = lax.rem(v, 2), lax.rem(lax.div(v, 2), 4), lax.div(v, 8)
    other = 1 - core

    def at_slab(d):
        return (lax.rem(s + d, 8), v)

    def at_x(d):
        return (s, lax.rem(x + d, 4) * 8 + zhi * 2 + core)

    def at_y(d):
        return (zlo * 4 + lax.rem(y + d, 4), v)

    def at_z(a, b):
        return (lax.rem(zlo + b, 2) * 4 + y, x * 8 + lax.rem(zhi + a, 4) * 2 + core)

    sibling = (s, x * 8 + zhi * 2 + other)
    z_peers = [(a, b) for a in range(4) for b in range(2) if a or b]

    used = [0]

    def send(src, dst, device):
        i = used[0]
        used[0] += 1
        copy = pltpu.make_async_remote_copy(
            src_ref=src, dst_ref=dst, send_sem=ssem.at[i], recv_sem=rsem.at[i],
            device_id=device, device_id_type=MESH,
        )
        copy.start()
        return copy

    sent = []

    def arrive(copies):
        for copy in copies:
            copy.wait_recv()
        sent.extend(copies)

    greet = [at_slab(d) for d in range(1, 8)] + [sibling] + [at_x(d) for d in range(1, 4)]
    greet += [at_z(a, b) for a, b in z_peers if a]
    barrier = pltpu.get_barrier_semaphore()
    for device in greet:
        pl.semaphore_signal(barrier, inc=1, device_id=device, device_id_type=MESH)
    pl.semaphore_wait(barrier, len(greet))

    mine = al(s * FB, FB)

    slabs = [send(slab_ref, xg.at[s], at_slab(d)) for d in range(1, 8)]
    xg[s] = slab_ref[...]
    students = []
    for d in range(1, 8):
        rows = al(lax.rem(s + d, 8) * 256, 256)
        students.append(send(table_ref.at[pl.ds(rows, 256), :], sx.at[0, :, pl.ds(mine, FB)], at_slab(d)))
    local = pltpu.make_async_copy(
        table_ref.at[pl.ds(al(s * 256, 256), 256), :], sx.at[0, :, pl.ds(mine, FB)], lsem.at[0]
    )
    local.start()
    duals = send(sdual_ref.at[s], sdb, sibling)

    ids = ids_ref[core]
    high, low = lax.div(ids, 128), lax.rem(ids, 128)
    found = jnp.zeros((128, 512), F32)
    step = 256
    for block in range(DUAL_ROWS // step):
        hot = (lax.broadcasted_iota(jnp.int32, (step, 512), 0) + block * step == high).astype(F32).astype(BF16)
        rest = dual_ref[block * step : (block + 1) * step, :]
        for _ in range(3):
            part = rest.astype(BF16)
            found += dot_first(part, hot)
            rest = rest - part.astype(F32)
    lane = lax.broadcasted_iota(jnp.int32, (128, 512), 0) == low
    row = jnp.sum(jnp.where(lane, found, 0.0), axis=0, keepdims=True)
    column = jnp.broadcast_to(row, (128, 512)).T
    rd[0] = column[:256]
    rd[1] = column[256:]

    arrive(slabs)
    for i in range(4):
        rows = slice((i % 2) * 128, (i % 2) * 128 + 128)
        csend[i // 2, rows, :] = dot(xg[other * 4 + i], proj_ref[...])
    pair = send(csend, crecv, sibling)
    for i in range(4):
        rows = slice((i % 2) * 128, (i % 2) * 128 + 128)
        acc[i // 2, rows, :] = dot(xg[core * 4 + i], proj_ref[...])
    arrive([pair])
    acc[...] += crecv[...]
    xsend[...] = acc[...].astype(BF16)
    copies = []
    for d in range(1, 4):
        rows = al(lax.rem(x + d, 4) * 64, 64)
        copies.append(send(xsend.at[:, pl.ds(rows, 64), :], xrecv.at[d - 1], at_x(d)))
    arrive(copies)
    total = acc[:, pl.ds(al(x * 64, 64), 64), :]
    for d in range(3):
        total += xrecv[d].astype(F32)
    zsend[...] = total
    copies = []
    for a in range(1, 4):
        rows = al(lax.rem(zhi + a, 4) * 16, 16)
        copies.append(send(zsend.at[:, pl.ds(rows, 16), :], zrecv.at[a - 1], at_z(a, 0)))
    arrive(copies)
    total = zsend[:, pl.ds(al(zhi * 16, 16), 16), :]
    for a in range(3):
        total += zrecv[a]
    pown[...] = total.astype(BF16)

    xrows = al(x * 64, 64)
    own_rows = al(x * 64 + zhi * 16, 16)
    copies = [send(pown, pbuf.at[:, pl.ds(own_rows, 16), pl.ds(mine, FB)], at_z(a, b)) for a, b in z_peers]
    keep = pltpu.make_async_copy(pown, pbuf.at[:, pl.ds(own_rows, 16), pl.ds(mine, FB)], lsem.at[1])
    keep.start()

    arrive(students)
    local.wait()
    both = send(sx.at[0], sx.at[1], sibling)

    keep.wait()
    arrive(copies)
    ycols = [al((z * 4 + y) * FB, FB) for z in range(2)]
    to_x, to_y = [], []
    for d in range(1, 4):
        for z in range(2):
            block = pbuf.at[0, pl.ds(xrows, 64), pl.ds(ycols[z], FB)]
            to_x.append(send(block, block, at_x(d)))
            block = pbuf.at[1, pl.ds(xrows, 64), pl.ds(ycols[z], FB)]
            to_y.append(send(block, block, at_y(d)))
    arrive(to_x)
    first = []
    for d in range(1, 4):
        for z in range(2):
            block = pbuf.at[0, :, pl.ds(ycols[z], FB)]
            first.append(send(block, block, at_y(d)))
    arrive(to_y)
    second = []
    for d in range(1, 4):
        block = pbuf.at[1, pl.ds(xrows, 64), :]
        second.append(send(block, block, at_x(d)))

    arrive([both, duals])
    for j in range(2):
        norm = jnp.zeros((256, 1), F32)
        for c in range(8):
            part = sx[j, :, c * FB : (c + 1) * FB].astype(F32)
            norm += jnp.sum(part * part, axis=1, keepdims=True)
        norm = jnp.broadcast_to(norm, (256, 128)).T[0:1]
        dual = sdual_ref[s] if j == 0 else sdb[...]
        qrow[j] = (dual - norm * (1.0 / DS)) * (1.0 / STRENGTH)

    def affinity(k):
        norm = jnp.zeros((256, 1), F32)
        for c in range(8):
            part = pbuf[k, :, c * FB : (c + 1) * FB].astype(F32)
            norm += jnp.sum(part * part, axis=1, keepdims=True)
        bias = (rd[k][:, 0:1] - norm * (1.0 / DS)) * (1.0 / STRENGTH)
        mass = jnp.zeros((256, 1), F32)
        for j in range(2):
            inner = dot_last(pbuf[k], sx[j])
            entry = jnp.exp(bias + qrow[j] + inner * (2.0 / (DS * STRENGTH))).astype(BF16)
            kb[k, j] = entry
            wide = entry.astype(F32)
            kt[k, j] = wide.T.astype(BF16)
            mass += jnp.sum(wide, axis=1, keepdims=True)

        @pl.loop(0, 8)
        def _(c):
            cols = pl.ds(al(c * FB, FB), FB)
            term = mass * pbuf[k, :, cols].astype(F32)
            term -= dot(kb[k, 0], sx[0, :, cols])
            term -= dot(kb[k, 1], sx[1, :, cols])
            rbuf[k, :, cols] = term.astype(BF16)

    arrive(first)
    affinity(0)
    to_y = []
    for d in range(1, 4):
        for z in range(2):
            cols = al((z * 4 + lax.rem(y + d, 4)) * FB, FB)
            to_y.append(send(rbuf.at[0, :, pl.ds(cols, FB)], ra1.at[d - 1, z], at_y(d)))
    arrive(second)
    affinity(1)
    to_x = []
    for d in range(1, 4):
        rows = al(lax.rem(x + d, 4) * 64, 64)
        to_x.append(send(rbuf.at[1, pl.ds(rows, 64), :], rb1.at[d - 1], at_x(d)))

    def student_term(j, cols, mass):
        term = mass * sx[j, :, cols].astype(F32)
        term -= dot(kt[0, j], pbuf[0, :, cols])
        return term - dot(kt[1, j], pbuf[1, :, cols])

    def student_mass(j):
        wide = kt[0, j].astype(F32) + kt[1, j].astype(F32)
        return jnp.sum(wide, axis=1, keepdims=True)

    mass1 = student_mass(1)

    @pl.loop(0, 8)
    def _(c):
        cols = pl.ds(al(c * FB, FB), FB)
        stsend[:, cols] = student_term(1, cols, mass1).astype(BF16)

    swap = send(stsend, strecv, sibling)
    mass0 = student_mass(0)

    @pl.loop(0, 8)
    def _(c):
        cols = pl.ds(al(c * FB, FB), FB)
        stown[:, cols] = student_term(0, cols, mass0)

    arrive(to_y)
    for z in range(2):
        total = rbuf[0, :, pl.ds(ycols[z], FB)].astype(F32)
        for d in range(3):
            total += ra1[d, z].astype(F32)
        ra2[z] = total.astype(BF16)
    to_x2 = []
    for d in range(1, 4):
        rows = al(lax.rem(x + d, 4) * 64, 64)
        to_x2.append(send(ra2.at[:, pl.ds(rows, 64), :], ra2r.at[d - 1], at_x(d)))
    arrive(to_x)
    total = rbuf[1, pl.ds(xrows, 64), :].astype(F32)
    for d in range(3):
        total += rb1[d].astype(F32)
    rb2[...] = total.astype(BF16)
    to_y2 = []
    for d in range(1, 4):
        for z in range(2):
            cols = al((z * 4 + lax.rem(y + d, 4)) * FB, FB)
            to_y2.append(send(rb2.at[:, pl.ds(cols, FB)], rb2r.at[d - 1, z], at_y(d)))

    arrive(to_x2)
    total = ra2[:, pl.ds(xrows, 64), :].astype(F32)
    for d in range(3):
        total += ra2r[d].astype(F32)
    rz[:, 0] = total.astype(BF16)
    arrive(to_y2)
    for z in range(2):
        total = rb2[:, pl.ds(ycols[z], FB)].astype(F32)
        for d in range(3):
            total += rb2r[d, z].astype(F32)
        rz[z, 1] = total.astype(BF16)
    copies = []
    for i, (a, b) in enumerate(z_peers):
        rows = al(lax.rem(zhi + a, 4) * 16, 16)
        copies.append(send(rz.at[lax.rem(zlo + b, 2), :, pl.ds(rows, 16), :], rzr.at[i], at_z(a, b)))

    arrive([swap])

    @pl.loop(0, 8)
    def _(c):
        cols = pl.ds(al(c * FB, FB), FB)
        gown[:, cols] = ((stown[:, cols] + strecv[:, cols].astype(F32)) * (1.0 / ROWS)).astype(BF16)

    arrive(copies)
    total = rz[zlo, :, pl.ds(al(zhi * 16, 16), 16), :].astype(F32)
    for i in range(7):
        total += rzr[i].astype(F32)
    rgown[...] = (total * (1.0 / VOCAB)).astype(BF16)
    copies = [send(rgown, rg.at[core, :, pl.ds(own_rows, 16), :], at_z(a, 0)) for a in range(1, 4)]
    rg[core, :, pl.ds(own_rows, 16), :] = rgown[...]

    srows = al(s * 256, 256)
    back = []
    for d in range(1, 8):
        cols = al(lax.rem(s + d, 8) * FB, FB)
        back.append(send(gown.at[:, pl.ds(cols, FB)], gst_ref.at[pl.ds(srows, 256), :], at_slab(d)))
    gst_ref[pl.ds(srows, 256), :] = gown[:, pl.ds(mine, FB)]

    arrive(copies)
    copies = []
    for d in range(1, 4):
        block = rg.at[core, :, pl.ds(xrows, 64), :]
        copies.append(send(block, block, at_x(d)))
    arrive(copies)
    pair = send(rg.at[core], rg.at[core], sibling)
    arrive([pair])

    def slab_term(index):
        half, k, rows = lax.div(index, 4), lax.rem(lax.div(index, 2), 2), al(lax.rem(index, 2) * 128, 128)
        return dot_last(rg[half, k, pl.ds(rows, 128), :], proj_ref[...])

    copies = []
    for d in range(1, 8):
        fsend[d - 1] = slab_term(lax.rem(s + d, 8)).astype(BF16)
        copies.append(send(fsend.at[d - 1], frecv.at[d - 1], at_slab(d)))
    own = slab_term(s)
    total = jnp.zeros((256, FB), F32)
    for i in range(8):
        half, k, rows = i // 4, (i // 2) % 2, (i % 2) * 128
        total += dot_first(xg[i], rg[half, k, rows : rows + 128, :])
    gp_ref[...] = (total * (1.0 / 32.0)).astype(BF16)
    arrive(copies)
    for d in range(7):
        own += frecv[d].astype(F32)
    gs_ref[...] = own.astype(BF16)

    arrive(back)
    for copy in sent:
        copy.wait_send()


def per_device(
    teacher_ids, slab_embed, projection, learner_vector_table, teacher_dual, student_dual
):
    ids = teacher_ids.reshape(2, 1, ROWS // 2)
    count = teacher_dual.shape[0]
    duals = jnp.pad(teacher_dual, (0, DUAL_ROWS * 128 - count)).reshape(DUAL_ROWS, 128)
    sdual = student_dual.reshape(8, 1, 256)
    vmem = pl.BlockSpec(memory_space=pltpu.VMEM)
    bf, ff = (lambda *n: pltpu.VMEM(n, BF16)), (lambda *n: pltpu.VMEM(n, F32))
    return pl.pallas_call(
        kernel,
        out_shape=(
            jax.ShapeDtypeStruct(projection.shape, BF16),
            jax.ShapeDtypeStruct(slab_embed.shape, BF16),
            jax.ShapeDtypeStruct(learner_vector_table.shape, BF16),
        ),
        in_specs=[vmem, vmem, vmem, pl.BlockSpec(memory_space=pl.ANY), vmem, vmem],
        out_specs=(vmem, vmem, vmem),
        scratch_shapes=[
            bf(8, 128, 256),
            bf(2, 256, DS),
            ff(1, 256),
            ff(2, 256, FB),
            ff(2, 256, FB),
            ff(2, 256, FB),
            bf(2, 256, FB),
            bf(3, 2, 64, FB),
            ff(2, 64, FB),
            ff(3, 2, 16, FB),
            bf(2, 16, FB),
            bf(2, 256, DS),
            ff(2, 256, 128),
            ff(2, 1, 256),
            bf(2, 2, 256, 256),
            bf(2, 2, 256, 256),
            bf(2, 256, DS),
            bf(3, 2, 256, FB),
            bf(3, 64, DS),
            bf(2, 256, FB),
            bf(64, DS),
            bf(3, 2, 64, FB),
            bf(3, 2, 64, FB),
            bf(2, 2, 64, FB),
            bf(7, 2, 16, FB),
            bf(2, 16, FB),
            bf(2, 2, 256, FB),
            bf(256, DS),
            bf(256, DS),
            ff(256, DS),
            bf(256, DS),
            bf(7, 128, 256),
            bf(7, 128, 256),
            pltpu.SemaphoreType.DMA((NSEM,)),
            pltpu.SemaphoreType.DMA((NSEM,)),
            pltpu.SemaphoreType.DMA((2,)),
        ],
        compiler_params=pltpu.CompilerParams(
            collective_id=0, has_side_effects=True, vmem_limit_bytes=56 * 1024 * 1024
        ),
        cost_estimate=pl.CostEstimate(flops=5_500_000_000, bytes_accessed=5_000_000, transcendentals=262144),
    )(ids, slab_embed, projection, learner_vector_table, duals, sdual)


def solution(mesh):
    in_specs = (P(), P("slab", "vocab"), P("vocab", "slab"), P("vocab", "slab"), P(), P("vocab"))
    out_specs = (P("vocab", "slab"), P("slab", "vocab"), P("vocab", "slab"))
    return jax.shard_map(
        per_device, mesh=mesh, in_specs=in_specs, out_specs=out_specs, check_vma=False
    )
```

```python
import jax
import jax.numpy as jnp
from jax import lax
from jax.experimental import pallas as pl
from jax.experimental.pallas import tpu as pltpu
from jax.sharding import PartitionSpec as P

DS = 3072
ROWS = 1024
VOCAB = 65536
STRENGTH = 0.04
FB = 384
NSEM = 224
IN_FIRST, IN_LATER = ((1, 1), (3, 1), (1, 0), (3, 0), (2, 0)), ((2, 1), (0, 1))
OUT_FIRST, OUT_THEN, OUT_LATER = ((1, 1), (3, 1)), ((1, 0), (3, 0), (2, 0)), ((2, 1), (0, 1))
F32, BF16 = jnp.float32, jnp.bfloat16
MESH = pl.DeviceIdType.MESH


def dot_last(a, b):
    return lax.dot_general(a, b, (((1,), (1,)), ((), ())), preferred_element_type=F32)


def dot_first(a, b):
    return lax.dot_general(a, b, (((0,), (0,)), ((), ())), preferred_element_type=F32)


def dot(a, b):
    return jnp.dot(a, b, preferred_element_type=F32)


def al(value, size):
    return pl.multiple_of(value, size)


def kernel(
    ids_ref, slab_ref, proj_hbm, table_ref, dual_hbm, sdual_ref,
    gp_ref, gs_ref, gst_ref,
    proj_ref, dual_ref, xg, sx, sdb, crecv, csend, acc, xsend, xrecv, zsend, zrecv, pown, pbuf,
    dtail, rd, qrow, kb, kt, rbuf, rfirst, rlast, rmid, rgot, rz, rzr,
    rgown, rg, stsend, strecv, stown, gown, fsend, frecv,
    ssem, rsem, lsem,
):
    s = lax.axis_index("slab")
    v = lax.axis_index("vocab")
    zlo, y = lax.div(s, 4), lax.rem(s, 4)
    core, zhi, x = lax.rem(v, 2), lax.rem(lax.div(v, 2), 4), lax.div(v, 8)
    other, zother = 1 - core, 1 - zlo

    def at_slab(d):
        return (lax.rem(s + d, 8), v)

    def at_x(d):
        return (s, lax.rem(x + d, 4) * 8 + zhi * 2 + core)

    def at_y(d):
        return (zlo * 4 + lax.rem(y + d, 4), v)

    def at_yz(d, b):
        return (lax.rem(zlo + b, 2) * 4 + lax.rem(y + d, 4), v)

    def at_z(a, b):
        return (lax.rem(zlo + b, 2) * 4 + y, x * 8 + lax.rem(zhi + a, 4) * 2 + core)

    sibling = (s, x * 8 + zhi * 2 + other)
    slab_order = [(1, 1), (3, 1), (2, 1), (1, 0), (3, 0), (2, 0), (0, 1)]
    z_peers = [(a, b) for a in range(4) for b in range(2) if a or b]

    used = [0]
    sent = []

    def send(src, dst, device):
        i = used[0]
        used[0] += 1
        copy = pltpu.make_async_remote_copy(
            src_ref=src, dst_ref=dst, send_sem=ssem.at[i], recv_sem=rsem.at[i],
            device_id=device, device_id_type=MESH,
        )
        copy.start()
        return copy

    def arrive(copies):
        for copy in copies:
            copy.wait_recv()
        sent.extend(copies)

    class Gather:
        def __init__(self, view, index, at):
            self.view, self.index, self.at = view, index, at
            a, b = view(index, 0), view(index, 1)
            self.first = [send(a, a, at(1)), send(b, b, at(3))]
            self.rest = [send(b, b, at(1)), send(a, a, at(3))]

        def forward(self):
            arrive(self.first[:1])
            block = self.view(lax.rem(self.index + 3, 4), 0)
            self.rest.append(send(block, block, self.at(1)))
            arrive(self.first[1:])
            block = self.view(lax.rem(self.index + 1, 4), 1)
            self.rest.append(send(block, block, self.at(3)))

        def finish(self):
            arrive(self.rest)

    class Reduce:
        def __init__(self, view, index, at, first, last, own=None):
            self.view, self.index, self.at, self.first, self.last = view, index, at, first, last
            self.own = own or (lambda j, h: view(j, h)[...].astype(F32))
            right, left, far = [lax.rem(index + d, 4) for d in (1, 3, 2)]
            self.right, self.left = right, left
            self.head = [send(view(far, 0), first.at[0], at(1)), send(view(far, 1), first.at[1], at(3))]
            self.rest = [send(view(right, 1), last.at[0, 1], at(1)), send(view(left, 0), last.at[1, 0], at(3))]

        def forward(self):
            arrive(self.head[:1])
            block = self.view(self.right, 0)
            block[...] = (self.own(self.right, 0) + self.first[0].astype(F32)).astype(BF16)
            self.rest.append(send(block, self.last.at[0, 0], self.at(1)))
            arrive(self.head[1:])
            block = self.view(self.left, 1)
            block[...] = (self.own(self.left, 1) + self.first[1].astype(F32)).astype(BF16)
            self.rest.append(send(block, self.last.at[1, 1], self.at(3)))

        def finish(self):
            arrive(self.rest)

        def total(self, h):
            total = self.own(self.index, h) + self.last[0, h].astype(F32)
            return total + self.last[1, h].astype(F32)

    class Spread:
        def __init__(self, block, at):
            self.copies = [send(block, block, at(d)) for d in (1, 3, 2)]

        def finish(self):
            arrive(self.copies)

    class Collect:
        def __init__(self, view, index, at, got):
            self.got = got
            self.copies = [send(view(lax.rem(index + d, 4)), got.at[d - 1], at(d)) for d in (1, 3, 2)]

        def total(self, own):
            arrive(self.copies)
            for d in range(3):
                own += self.got[d].astype(F32)
            return own

    greet = [at_slab(d) for d in range(1, 8)] + [sibling] + [at_x(d) for d in (1, 2, 3)]
    greet += [at_z(a, b) for a, b in z_peers if a]
    barrier = pltpu.get_barrier_semaphore()
    for device in greet:
        pl.semaphore_signal(barrier, inc=1, device_id=device, device_id_type=MESH)
    pl.semaphore_wait(barrier, len(greet))

    mine = al(s * FB, FB)
    own_rows = pl.ds(al(zhi * 16, 16), 16)

    def yz(d, b):
        return lax.rem(zlo + b, 2) * 4 + lax.rem(y + d, 4)

    state = {}
    load_proj = pltpu.make_async_copy(proj_hbm, proj_ref, lsem.at[2])
    load_dual = pltpu.make_async_copy(dual_hbm, dual_ref, lsem.at[3])
    load_proj.start()
    load_dual.start()

    def rows_of(ref, k, c, u):
        return ref[k, c // 4, c % 4, :, u * 32 : u * 32 + 32, :].reshape(128, FB)

    def affinity(k, u):
        norm = jnp.zeros((128, 1), F32)
        for c in range(8):
            part = rows_of(pbuf, k, c, u).astype(F32)
            norm += jnp.sum(part * part, axis=1, keepdims=True)
        bias = rd[k, :, u * 32 : u * 32 + 32, 0:1].reshape(128, 1)
        bias = (bias - norm * (1.0 / DS)) * (1.0 / STRENGTH)
        mass = jnp.zeros((128, 1), F32)
        for j in range(2):
            inner = jnp.zeros((128, 256), F32)
            for c in range(8):
                inner += dot_last(rows_of(pbuf, k, c, u), sx[j, :, c * FB : (c + 1) * FB])
            entry = jnp.exp(bias + qrow[j] + inner * (2.0 / (DS * STRENGTH))).astype(BF16)
            kb[j] = entry
            wide = entry.astype(F32)
            kt[k, j, :, u * 128 : u * 128 + 128] = wide.T.astype(BF16)
            mass += jnp.sum(wide, axis=1, keepdims=True)
        for c in range(8):
            cols = slice(c * FB, (c + 1) * FB)
            term = mass * rows_of(pbuf, k, c, u).astype(F32)
            term -= dot(kb[0], sx[0, :, cols])
            term -= dot(kb[1], sx[1, :, cols])
            rbuf[k, c // 4, c % 4, :, u * 32 : u * 32 + 32, :] = term.astype(BF16).reshape(4, 32, FB)

    def slab_term(k, index):
        return dot_last(rg[lax.div(index, 4), k, lax.rem(index, 4)], proj_ref[...])

    def chain(k):
        index_mid, at_mid, index_last, at_last = (x, at_x, y, at_y) if k == 0 else (y, at_y, x, at_x)

        def block_of(ref, u):
            def view(j, h):
                rows = slice(u * 32 + h * 16, u * 32 + h * 16 + 16)
                return ref.at[0, :, j, :, rows, :] if k == 0 else ref.at[1, :, :, j, rows, :]

            return view

        whole = slice(k * 64, k * 64 + 64)
        copies = [send(slab_ref.at[whole, :], xg.at[s, whole, :], at_yz(d, b)) for d, b in slab_order]
        xg[s, whole, :] = slab_ref[whole, :]
        yield
        arrive(copies)
        if k == 0:
            load_proj.wait()
        for i in range(4):
            csend[k, i] = dot(xg[other * 4 + i, whole, :], proj_ref[...])
        pair = send(csend.at[k], crecv.at[k], sibling)
        for i in range(4):
            acc[k, i] = dot(xg[core * 4 + i, whole, :], proj_ref[...])
        yield
        arrive([pair])
        acc[k] = acc[k] + crecv[k]
        xsend[k] = acc[k].astype(BF16)
        collect = Collect(lambda j: xsend.at[k, j], x, at_x, xrecv.at[k])
        yield
        zsend[k] = collect.total(acc[k, x])
        copies = []
        for a in range(1, 4):
            rows = al(lax.rem(zhi + a, 4) * 16, 16)
            copies.append(send(zsend.at[k, pl.ds(rows, 16), :], zrecv.at[k, a - 1], at_z(a, 0)))
        yield
        arrive(copies)
        total = zsend[k, own_rows, :]
        for a in range(3):
            total += zrecv[k, a]
        pown[k] = total.astype(BF16)
        place = pbuf.at[k, zlo, y, x, own_rows, :]
        copies = [send(pown.at[k], place, at_z(a, b)) for a, b in z_peers]
        pbuf[k, zlo, y, x, own_rows, :] = pown[k]
        yield
        arrive(copies)
        spread = Spread(pbuf.at[k, :, y, x], at_mid)
        yield
        spread.finish()
        gathers = [Gather(block_of(pbuf, u), index_last, at_last) for u in range(2)]
        yield
        gathers[0].forward()
        yield
        gathers[1].forward()
        yield
        reduces = []
        for u in range(2):
            gathers[u].finish()
            affinity(k, u)
            reduces.append(Reduce(block_of(rbuf, u), index_last, at_last, rfirst.at[k, u], rlast.at[k, u]))
            yield
        reduces[0].forward()
        yield
        reduces[1].forward()
        yield
        for u in range(2):
            reduces[u].finish()
            for h in range(2):
                rmid[k, :, :, u * 32 + h * 16 : u * 32 + h * 16 + 16, :] = reduces[u].total(h).astype(BF16)
        collect = Collect(lambda j: rmid.at[k, :, j], index_mid, at_mid, rgot.at[k])
        yield
        rz[k] = collect.total(rmid[k, :, index_mid].astype(F32)).astype(BF16)
        copies = []
        for i, (a, b) in enumerate(z_peers):
            rows = al(lax.rem(zhi + a, 4) * 16, 16)
            copies.append(send(rz.at[k, lax.rem(zlo + b, 2), pl.ds(rows, 16), :], rzr.at[k, i], at_z(a, b)))
        yield
        arrive(copies)
        total = rz[k, zlo, own_rows, :].astype(F32)
        for i in range(7):
            total += rzr[k, i].astype(F32)
        rgown[k] = (total * (1.0 / VOCAB)).astype(BF16)
        copies = [send(rgown.at[k], rg.at[core, k, x, own_rows, :], at_z(a, 0)) for a in range(1, 4)]
        rg[core, k, x, own_rows, :] = rgown[k]
        yield
        arrive(copies)
        spread = Spread(rg.at[core, k, x], at_x)
        yield
        spread.finish()
        pair = send(rg.at[core, k], rg.at[core, k], sibling)
        yield
        arrive([pair])
        copies = []
        for i, (d, b) in enumerate(slab_order):
            fsend[k, i] = slab_term(k, yz(d, b)).astype(BF16)
            copies.append(send(fsend.at[k, i], frecv.at[k, i], at_yz(d, b)))
        yield
        total = slab_term(k, s)
        arrive(copies)
        for i in range(7):
            total += frecv[k, i].astype(F32)
        gs_ref[whole, :] = total.astype(BF16)
        yield

    def student_block(d, b):
        rows = al(yz(d, b) * 256, 256)
        return send(table_ref.at[pl.ds(rows, 256), :], sx.at[0, :, pl.ds(mine, FB)], at_yz(d, b))

    def students_start():
        state["students"] = [student_block(d, b) for d, b in IN_FIRST]
        state["local"] = pltpu.make_async_copy(
            table_ref.at[pl.ds(al(s * 256, 256), 256), :], sx.at[0, :, pl.ds(mine, FB)], lsem.at[0]
        )
        state["local"].start()
        state["duals"] = send(sdual_ref.at[s], sdb, sibling)

    def students_across():
        state["students"] += [student_block(d, b) for d, b in IN_LATER]

    def students_swap():
        arrive(state["students"])
        state["local"].wait()
        state["both"] = send(sx.at[0], sx.at[1], sibling)

    def teacher_duals():
        ids = ids_ref[core]
        high, low = lax.div(ids, 128), lax.rem(ids, 128)
        found = jnp.zeros((128, 512), F32)
        load_dual.wait()
        dtail[...] = jnp.zeros_like(dtail)
        whole = dual_ref.shape[0] // 16 * 16
        dtail[0 : dual_ref.shape[0] - whole, :] = dual_ref[whole:, :]
        half = whole // 2
        for base, rest in ((0, dual_ref[0:half, :]), (half, dual_ref[half:whole, :]), (whole, dtail[...])):
            hot = lax.broadcasted_iota(jnp.int32, (rest.shape[0], 512), 0) + base == high
            hot = hot.astype(F32).astype(BF16)
            for _ in range(3):
                part = rest.astype(BF16)
                found += dot_first(part, hot)
                rest = rest - part.astype(F32)
        lane = lax.broadcasted_iota(jnp.int32, (128, 512), 0) == low
        row = jnp.sum(jnp.where(lane, found, 0.0), axis=0, keepdims=True)
        column = jnp.broadcast_to(row, (128, 512)).T
        for k in range(2):
            for i in range(4):
                rd[k, i] = column[i * 128 + k * 64 : i * 128 + k * 64 + 64]

    def student_norms():
        arrive([state["both"], state["duals"]])
        for j in range(2):
            norm = jnp.zeros((256, 1), F32)
            for c in range(8):
                part = sx[j, :, c * FB : (c + 1) * FB].astype(F32)
                norm += jnp.sum(part * part, axis=1, keepdims=True)
            norm = jnp.broadcast_to(norm, (256, 128)).T[0:1]
            dual = sdual_ref[s] if j == 0 else sdb[...]
            qrow[j] = (dual - norm * (1.0 / DS)) * (1.0 / STRENGTH)

    def student_term(j, c, mass):
        cols = slice(c * FB, (c + 1) * FB)
        term = mass * sx[j, :, cols].astype(F32)
        for k in range(2):
            rows = jnp.concatenate([rows_of(pbuf, k, c, u) for u in range(2)], axis=0)
            term -= dot(kt[k, j], rows)
        return cols, term

    def student_mass(j):
        wide = kt[0, j].astype(F32) + kt[1, j].astype(F32)
        return jnp.sum(wide, axis=1, keepdims=True)

    def student_swap():
        mass = student_mass(1)

        for c in range(8):
            cols, term = student_term(1, c, mass)
            stsend[:, cols] = term.astype(BF16)

        state["swap"] = send(stsend, strecv, sibling)

    def student_own():
        mass = student_mass(0)

        for c in range(8):
            cols, term = student_term(0, c, mass)
            stown[:, cols] = term

    srows = al(s * 256, 256)

    def student_out(places):
        for d, b in places:
            cols = pl.ds(al(yz(d, b) * FB, FB), FB)
            state["back"].append(
                send(gown.at[:, cols], gst_ref.at[pl.ds(srows, 256), :], at_yz(d, b))
            )

    def student_back():
        arrive([state["swap"]])

        @pl.loop(0, 8)
        def _(c):
            cols = pl.ds(al(c * FB, FB), FB)
            gown[:, cols] = ((stown[:, cols] + strecv[:, cols].astype(F32)) * (1.0 / ROWS)).astype(BF16)

        state["back"] = []
        student_out(OUT_FIRST)
        state["keep"] = pltpu.make_async_copy(
            gown.at[:, pl.ds(mine, FB)], gst_ref.at[pl.ds(srows, 256), :], lsem.at[1]
        )
        state["keep"].start()

    def projection_gradient():
        total = jnp.zeros((256, FB), F32)
        for i in range(8):
            grad = jnp.concatenate([rg[i // 4, 0, i % 4], rg[i // 4, 1, i % 4]], axis=0)
            total += dot_first(xg[i], grad)
        gp_ref[...] = (total * (1.0 / 32.0)).astype(BF16)

    aside = {
        1: [students_start],
        2: [teacher_duals],
        5: [students_across],
        6: [students_swap],
        8: [student_norms],
        10: [student_swap],
        11: [student_own, student_back],
        14: [lambda: student_out(OUT_THEN)],
        16: [lambda: student_out(OUT_LATER)],
        18: [projection_gradient],
    }
    chains = [chain(0), chain(1)]
    for stage in range(20):
        for one in chains:
            next(one)
        for work in aside.get(stage, []):
            work()

    arrive(state["back"])
    state["keep"].wait()
    for copy in sent:
        copy.wait_send()


def deliver(gp_in, gs_in, gst_in, gp_ref, gs_ref, gst_ref, gp, gs, gst, sem):
    moves = [(gp_in, gp, gp_ref), (gs_in, gs, gs_ref)]
    part = gst_in.shape[0] // 4
    for i in range(4):
        rows = pl.ds(i * part, part)
        moves.append((gst_in.at[rows], gst.at[rows], gst_ref.at[rows]))
    loads = [pltpu.make_async_copy(a, b, sem.at[0, i]) for i, (a, b, _) in enumerate(moves)]
    stores = [pltpu.make_async_copy(b, c, sem.at[1, i]) for i, (_, b, c) in enumerate(moves)]
    for load in loads:
        load.start()
    for load, store in zip(loads, stores):
        load.wait()
        store.start()
    for store in stores:
        store.wait()


def per_device(
    teacher_ids, slab_embed, projection, learner_vector_table, teacher_dual, student_dual
):
    ids = teacher_ids.reshape(2, 1, ROWS // 2)
    duals = teacher_dual.reshape(teacher_dual.shape[0] // 128, 128)
    sdual = student_dual.reshape(8, 1, 256)
    vmem = pl.BlockSpec(memory_space=pltpu.VMEM)
    bf, ff = (lambda *n: pltpu.VMEM(n, BF16)), (lambda *n: pltpu.VMEM(n, F32))
    anywhere = pl.BlockSpec(memory_space=pl.ANY)
    shapes = (
        jax.ShapeDtypeStruct(projection.shape, BF16),
        jax.ShapeDtypeStruct(slab_embed.shape, BF16),
        jax.ShapeDtypeStruct(learner_vector_table.shape, BF16),
    )
    results = pl.pallas_call(
        kernel,
        out_shape=shapes,
        in_specs=[vmem, vmem, anywhere, anywhere, anywhere, vmem],
        out_specs=(vmem, vmem, anywhere),
        scratch_shapes=[
            pltpu.VMEM(projection.shape, BF16),
            pltpu.VMEM(duals.shape, F32),
            bf(8, 128, 256),
            bf(2, 256, DS),
            ff(1, 256),
            ff(2, 4, 64, FB),
            ff(2, 4, 64, FB),
            ff(2, 4, 64, FB),
            bf(2, 4, 64, FB),
            bf(2, 3, 64, FB),
            ff(2, 64, FB),
            ff(2, 3, 16, FB),
            bf(2, 16, FB),
            bf(2, 2, 4, 4, 64, FB),
            ff(16, 128),
            ff(2, 4, 64, 128),
            ff(2, 1, 256),
            bf(2, 128, 256),
            bf(2, 2, 256, 256),
            bf(2, 2, 4, 4, 64, FB),
            bf(2, 2, 2, 2, 4, 16, FB),
            bf(2, 2, 2, 2, 2, 4, 16, FB),
            bf(2, 2, 4, 64, FB),
            bf(2, 3, 2, 64, FB),
            bf(2, 2, 64, FB),
            bf(2, 7, 16, FB),
            bf(2, 16, FB),
            bf(2, 2, 4, 64, FB),
            bf(256, DS),
            bf(256, DS),
            ff(256, DS),
            bf(256, DS),
            bf(2, 7, 64, 256),
            bf(2, 7, 64, 256),
            pltpu.SemaphoreType.DMA((NSEM,)),
            pltpu.SemaphoreType.DMA((NSEM,)),
            pltpu.SemaphoreType.DMA((4,)),
        ],
        compiler_params=pltpu.CompilerParams(
            collective_id=0, has_side_effects=True, vmem_limit_bytes=56 * 1024 * 1024
        ),
        cost_estimate=pl.CostEstimate(flops=5_500_000_000, bytes_accessed=5_000_000, transcendentals=262144),
    )(ids, slab_embed, projection, learner_vector_table, duals, sdual)
    return pl.pallas_call(
        deliver,
        out_shape=shapes,
        in_specs=[anywhere] * 3,
        out_specs=(anywhere,) * 3,
        scratch_shapes=[pltpu.VMEM(shape.shape, BF16) for shape in shapes] + [pltpu.SemaphoreType.DMA((2, 6))],
        compiler_params=pltpu.CompilerParams(vmem_limit_bytes=60 * 1024 * 1024),
    )(*results)


def solution(mesh):
    in_specs = (P(), P("slab", "vocab"), P("vocab", "slab"), P("vocab", "slab"), P(), P("vocab"))
    out_specs = (P("vocab", "slab"), P("slab", "vocab"), P("vocab", "slab"))
    return jax.shard_map(
        per_device, mesh=mesh, in_specs=in_specs, out_specs=out_specs, check_vma=False
    )
```

```python
import jax
import jax.numpy as jnp
from jax import lax
from jax.experimental import pallas as pl
from jax.experimental.pallas import tpu as pltpu
from jax.sharding import PartitionSpec as P

DS = 3072
ROWS = 1024
VOCAB = 65536
STRENGTH = 0.04
FB = 384
NSEM = 224
IN_FIRST, IN_LATER = ((1, 1), (3, 1), (1, 0), (3, 0), (2, 0)), ((2, 1), (0, 1))
OUT_FIRST, OUT_THEN, OUT_LATER = ((1, 1), (3, 1)), ((1, 0), (3, 0), (2, 0)), ((2, 1), (0, 1))
F32, BF16 = jnp.float32, jnp.bfloat16
MESH = pl.DeviceIdType.MESH


def dot_last(a, b):
    return lax.dot_general(a, b, (((1,), (1,)), ((), ())), preferred_element_type=F32)


def dot_first(a, b):
    return lax.dot_general(a, b, (((0,), (0,)), ((), ())), preferred_element_type=F32)


def dot(a, b):
    return jnp.dot(a, b, preferred_element_type=F32)


def al(value, size):
    return pl.multiple_of(value, size)


def kernel(
    ids_ref, slab_ref, proj_hbm, table_ref, dual_hbm, sdual_ref,
    gp_ref, gs_ref, gst_ref,
    proj_ref, dual_ref, xg, sx, sdb, crecv, csend, acc, xsend, xrecv, zsend, zrecv, pown, pbuf,
    dtail, rd, qrow, kb, kt, rbuf, rfirst, rlast, rmid, rgot, rz, rzr,
    rgown, rg, stsend, strecv, stown, gown, fsend, frecv,
    ssem, rsem, lsem,
):
    s = lax.axis_index("slab")
    v = lax.axis_index("vocab")
    zlo, y = lax.div(s, 4), lax.rem(s, 4)
    core, zhi, x = lax.rem(v, 2), lax.rem(lax.div(v, 2), 4), lax.div(v, 8)
    other, zother = 1 - core, 1 - zlo

    def at_slab(d):
        return (lax.rem(s + d, 8), v)

    def at_x(d):
        return (s, lax.rem(x + d, 4) * 8 + zhi * 2 + core)

    def at_y(d):
        return (zlo * 4 + lax.rem(y + d, 4), v)

    def at_yz(d, b):
        return (lax.rem(zlo + b, 2) * 4 + lax.rem(y + d, 4), v)

    def at_z(a, b):
        return (lax.rem(zlo + b, 2) * 4 + y, x * 8 + lax.rem(zhi + a, 4) * 2 + core)

    sibling = (s, x * 8 + zhi * 2 + other)
    slab_order = [(1, 1), (3, 1), (2, 1), (1, 0), (3, 0), (2, 0), (0, 1)]
    z_peers = [(a, b) for a in range(4) for b in range(2) if a or b]

    used = [0]
    sent = []

    def send(src, dst, device):
        i = used[0]
        used[0] += 1
        copy = pltpu.make_async_remote_copy(
            src_ref=src, dst_ref=dst, send_sem=ssem.at[i], recv_sem=rsem.at[i],
            device_id=device, device_id_type=MESH,
        )
        copy.start()
        return copy

    def arrive(copies):
        for copy in copies:
            copy.wait_recv()
        sent.extend(copies)

    class Gather:
        def __init__(self, view, index, at):
            self.view, self.index, self.at = view, index, at
            a, b = view(index, 0), view(index, 1)
            self.first = [send(a, a, at(1)), send(b, b, at(3))]
            self.rest = [send(b, b, at(1)), send(a, a, at(3))]

        def forward(self):
            arrive(self.first[:1])
            block = self.view(lax.rem(self.index + 3, 4), 0)
            self.rest.append(send(block, block, self.at(1)))
            arrive(self.first[1:])
            block = self.view(lax.rem(self.index + 1, 4), 1)
            self.rest.append(send(block, block, self.at(3)))

        def finish(self):
            arrive(self.rest)

    class Reduce:
        def __init__(self, view, index, at, first, last, own=None):
            self.view, self.index, self.at, self.first, self.last = view, index, at, first, last
            self.own = own or (lambda j, h: view(j, h)[...].astype(F32))
            right, left, far = [lax.rem(index + d, 4) for d in (1, 3, 2)]
            self.right, self.left = right, left
            self.head = [send(view(far, 0), first.at[0], at(1)), send(view(far, 1), first.at[1], at(3))]
            self.rest = [send(view(right, 1), last.at[0, 1], at(1)), send(view(left, 0), last.at[1, 0], at(3))]

        def forward(self):
            arrive(self.head[:1])
            block = self.view(self.right, 0)
            block[...] = (self.own(self.right, 0) + self.first[0].astype(F32)).astype(BF16)
            self.rest.append(send(block, self.last.at[0, 0], self.at(1)))
            arrive(self.head[1:])
            block = self.view(self.left, 1)
            block[...] = (self.own(self.left, 1) + self.first[1].astype(F32)).astype(BF16)
            self.rest.append(send(block, self.last.at[1, 1], self.at(3)))

        def finish(self):
            arrive(self.rest)

        def total(self, h):
            total = self.own(self.index, h) + self.last[0, h].astype(F32)
            return total + self.last[1, h].astype(F32)

    class Spread:
        def __init__(self, block, at):
            self.copies = [send(block, block, at(d)) for d in (1, 3, 2)]

        def finish(self):
            arrive(self.copies)

    class Collect:
        def __init__(self, view, index, at, got):
            self.got = got
            self.copies = [send(view(lax.rem(index + d, 4)), got.at[d - 1], at(d)) for d in (1, 3, 2)]

        def total(self, own):
            arrive(self.copies)
            for d in range(3):
                own += self.got[d].astype(F32)
            return own

    greet = [at_slab(d) for d in range(1, 8)] + [sibling] + [at_x(d) for d in (1, 2, 3)]
    greet += [at_z(a, b) for a, b in z_peers if a]
    barrier = pltpu.get_barrier_semaphore()
    for device in greet:
        pl.semaphore_signal(barrier, inc=1, device_id=device, device_id_type=MESH)
    pl.semaphore_wait(barrier, len(greet))

    mine = al(s * FB, FB)
    own_rows = pl.ds(al(zhi * 16, 16), 16)

    def yz(d, b):
        return lax.rem(zlo + b, 2) * 4 + lax.rem(y + d, 4)

    state = {}
    load_proj = pltpu.make_async_copy(proj_hbm, proj_ref, lsem.at[2])
    load_dual = pltpu.make_async_copy(dual_hbm, dual_ref, lsem.at[3])
    load_proj.start()
    load_dual.start()

    def rows_of(ref, k, c, u):
        rows = slice(u * 32, u * 32 + 32)
        pair = [ref[k, i // 4, i % 4, :, rows, :].reshape(128, FB) for i in (2 * c, 2 * c + 1)]
        return jnp.concatenate(pair, axis=1)

    def affinity(k, u):
        norm = jnp.zeros((128, 1), F32)
        for c in range(4):
            part = rows_of(pbuf, k, c, u).astype(F32)
            norm += jnp.sum(part * part, axis=1, keepdims=True)
        bias = rd[k, :, u * 32 : u * 32 + 32, 0:1].reshape(128, 1)
        bias = (bias - norm * (1.0 / DS)) * (1.0 / STRENGTH)
        mass = jnp.zeros((128, 1), F32)
        for j in range(2):
            inner = jnp.zeros((128, 256), F32)
            for c in range(4):
                inner += dot_last(rows_of(pbuf, k, c, u), sx[j, :, c * 2 * FB : (c + 1) * 2 * FB])
            entry = jnp.exp(bias + qrow[j] + inner * (2.0 / (DS * STRENGTH))).astype(BF16)
            kb[j] = entry
            wide = entry.astype(F32)
            kt[k, j, :, u * 128 : u * 128 + 128] = wide.T.astype(BF16)
            mass += jnp.sum(wide, axis=1, keepdims=True)
        for c in range(4):
            cols = slice(c * 2 * FB, (c + 1) * 2 * FB)
            term = mass * rows_of(pbuf, k, c, u).astype(F32)
            term -= dot(kb[0], sx[0, :, cols])
            term -= dot(kb[1], sx[1, :, cols])
            for i in range(2):
                part = term[:, i * FB : (i + 1) * FB].astype(BF16).reshape(4, 32, FB)
                rbuf[k, (2 * c + i) // 4, (2 * c + i) % 4, :, u * 32 : u * 32 + 32, :] = part

    def slab_term(k, index):
        return dot_last(rg[lax.div(index, 4), k, lax.rem(index, 4)], proj_ref[...])

    def chain(k):
        index_mid, at_mid, index_last, at_last = (x, at_x, y, at_y) if k == 0 else (y, at_y, x, at_x)

        def block_of(ref, u):
            def view(j, h):
                rows = slice(u * 32 + h * 16, u * 32 + h * 16 + 16)
                return ref.at[0, :, j, :, rows, :] if k == 0 else ref.at[1, :, :, j, rows, :]

            return view

        whole = slice(k * 64, k * 64 + 64)
        copies = [send(slab_ref.at[whole, :], xg.at[s, whole, :], at_yz(d, b)) for d, b in slab_order]
        xg[s, whole, :] = slab_ref[whole, :]
        yield
        arrive(copies)
        if k == 0:
            load_proj.wait()
        for i in range(4):
            csend[k, i] = dot(xg[other * 4 + i, whole, :], proj_ref[...])
        pair = send(csend.at[k], crecv.at[k], sibling)
        for i in range(4):
            acc[k, i] = dot(xg[core * 4 + i, whole, :], proj_ref[...])
        yield
        arrive([pair])
        acc[k] = acc[k] + crecv[k]
        xsend[k] = acc[k].astype(BF16)
        collect = Collect(lambda j: xsend.at[k, j], x, at_x, xrecv.at[k])
        yield
        zsend[k] = collect.total(acc[k, x]).astype(BF16)
        copies = []
        for a in range(1, 4):
            rows = al(lax.rem(zhi + a, 4) * 16, 16)
            copies.append(send(zsend.at[k, pl.ds(rows, 16), :], zrecv.at[k, a - 1], at_z(a, 0)))
        yield
        arrive(copies)
        total = zsend[k, own_rows, :].astype(F32)
        for a in range(3):
            total += zrecv[k, a].astype(F32)
        pown[k] = total.astype(BF16)
        place = pbuf.at[k, zlo, y, x, own_rows, :]
        copies = [send(pown.at[k], place, at_z(a, b)) for a, b in z_peers]
        pbuf[k, zlo, y, x, own_rows, :] = pown[k]
        yield
        arrive(copies)
        spread = Spread(pbuf.at[k, :, y, x], at_mid)
        yield
        spread.finish()
        gathers = [Gather(block_of(pbuf, u), index_last, at_last) for u in range(2)]
        yield
        gathers[0].forward()
        yield
        gathers[1].forward()
        yield
        reduces = []
        for u in range(2):
            gathers[u].finish()
            affinity(k, u)
            reduces.append(Reduce(block_of(rbuf, u), index_last, at_last, rfirst.at[k, u], rlast.at[k, u]))
            yield
        reduces[0].forward()
        yield
        reduces[1].forward()
        yield
        for u in range(2):
            reduces[u].finish()
            for h in range(2):
                rmid[k, :, :, u * 32 + h * 16 : u * 32 + h * 16 + 16, :] = reduces[u].total(h).astype(BF16)
        collect = Collect(lambda j: rmid.at[k, :, j], index_mid, at_mid, rgot.at[k])
        yield
        rz[k] = collect.total(rmid[k, :, index_mid].astype(F32)).astype(BF16)
        copies = []
        for i, (a, b) in enumerate(z_peers):
            rows = al(lax.rem(zhi + a, 4) * 16, 16)
            copies.append(send(rz.at[k, lax.rem(zlo + b, 2), pl.ds(rows, 16), :], rzr.at[k, i], at_z(a, b)))
        yield
        arrive(copies)
        total = rz[k, zlo, own_rows, :].astype(F32)
        for i in range(7):
            total += rzr[k, i].astype(F32)
        rgown[k] = (total * (1.0 / VOCAB)).astype(BF16)
        copies = [send(rgown.at[k], rg.at[core, k, x, own_rows, :], at_z(a, 0)) for a in range(1, 4)]
        rg[core, k, x, own_rows, :] = rgown[k]
        yield
        arrive(copies)
        spread = Spread(rg.at[core, k, x], at_x)
        yield
        spread.finish()
        pair = send(rg.at[core, k], rg.at[core, k], sibling)
        yield
        arrive([pair])
        copies = []
        for i, (d, b) in enumerate(slab_order):
            fsend[k, i] = slab_term(k, yz(d, b)).astype(BF16)
            copies.append(send(fsend.at[k, i], frecv.at[k, i], at_yz(d, b)))
        yield
        total = slab_term(k, s)
        arrive(copies)
        for i in range(7):
            total += frecv[k, i].astype(F32)
        gs_ref[whole, :] = total.astype(BF16)
        yield

    def student_block(d, b):
        rows = al(yz(d, b) * 256, 256)
        return send(table_ref.at[pl.ds(rows, 256), :], sx.at[0, :, pl.ds(mine, FB)], at_yz(d, b))

    def students_start():
        state["students"] = [student_block(d, b) for d, b in IN_FIRST]
        state["local"] = pltpu.make_async_copy(
            table_ref.at[pl.ds(al(s * 256, 256), 256), :], sx.at[0, :, pl.ds(mine, FB)], lsem.at[0]
        )
        state["local"].start()
        state["duals"] = send(sdual_ref.at[s], sdb, sibling)

    def students_across():
        state["students"] += [student_block(d, b) for d, b in IN_LATER]

    def students_swap():
        arrive(state["students"])
        state["local"].wait()
        state["both"] = send(sx.at[0], sx.at[1], sibling)

    def teacher_duals():
        ids = ids_ref[core]
        high, low = lax.div(ids, 128), lax.rem(ids, 128)
        found = jnp.zeros((128, 512), F32)
        load_dual.wait()
        dtail[...] = jnp.zeros_like(dtail)
        whole = dual_ref.shape[0] // 16 * 16
        dtail[0 : dual_ref.shape[0] - whole, :] = dual_ref[whole:, :]
        half = whole // 2
        for base, rest in ((0, dual_ref[0:half, :]), (half, dual_ref[half:whole, :]), (whole, dtail[...])):
            hot = lax.broadcasted_iota(jnp.int32, (rest.shape[0], 512), 0) + base == high
            hot = hot.astype(F32).astype(BF16)
            for _ in range(3):
                part = rest.astype(BF16)
                found += dot_first(part, hot)
                rest = rest - part.astype(F32)
        lane = lax.broadcasted_iota(jnp.int32, (128, 512), 0) == low
        row = jnp.sum(jnp.where(lane, found, 0.0), axis=0, keepdims=True)
        column = jnp.broadcast_to(row, (128, 512)).T
        for k in range(2):
            for i in range(4):
                rd[k, i] = column[i * 128 + k * 64 : i * 128 + k * 64 + 64]

    def student_norms():
        arrive([state["both"], state["duals"]])
        for j in range(2):
            norm = jnp.zeros((256, 1), F32)
            for c in range(8):
                part = sx[j, :, c * FB : (c + 1) * FB].astype(F32)
                norm += jnp.sum(part * part, axis=1, keepdims=True)
            norm = jnp.broadcast_to(norm, (256, 128)).T[0:1]
            dual = sdual_ref[s] if j == 0 else sdb[...]
            qrow[j] = (dual - norm * (1.0 / DS)) * (1.0 / STRENGTH)

    def student_term(j, c, mass):
        cols = slice(c * 2 * FB, (c + 1) * 2 * FB)
        term = mass * sx[j, :, cols].astype(F32)
        for k in range(2):
            rows = jnp.concatenate([rows_of(pbuf, k, c, u) for u in range(2)], axis=0)
            term -= dot(kt[k, j], rows)
        return cols, term

    def student_mass(j):
        wide = kt[0, j].astype(F32) + kt[1, j].astype(F32)
        return jnp.sum(wide, axis=1, keepdims=True)

    def student_swap():
        mass = student_mass(1)

        for c in range(4):
            cols, term = student_term(1, c, mass)
            stsend[:, cols] = term.astype(BF16)

        state["swap"] = send(stsend, strecv, sibling)

    def student_own():
        mass = student_mass(0)

        for c in range(4):
            cols, term = student_term(0, c, mass)
            stown[:, cols] = term

    srows = al(s * 256, 256)

    def student_out(places):
        for d, b in places:
            cols = pl.ds(al(yz(d, b) * FB, FB), FB)
            state["back"].append(
                send(gown.at[:, cols], gst_ref.at[pl.ds(srows, 256), :], at_yz(d, b))
            )

    def student_back():
        arrive([state["swap"]])

        @pl.loop(0, 8)
        def _(c):
            cols = pl.ds(al(c * FB, FB), FB)
            gown[:, cols] = ((stown[:, cols] + strecv[:, cols].astype(F32)) * (1.0 / ROWS)).astype(BF16)

        state["back"] = []
        student_out(OUT_FIRST)
        state["keep"] = pltpu.make_async_copy(
            gown.at[:, pl.ds(mine, FB)], gst_ref.at[pl.ds(srows, 256), :], lsem.at[1]
        )
        state["keep"].start()

    def projection_gradient():
        total = jnp.zeros((256, FB), F32)
        for i in range(8):
            grad = jnp.concatenate([rg[i // 4, 0, i % 4], rg[i // 4, 1, i % 4]], axis=0)
            total += dot_first(xg[i], grad)
        gp_ref[...] = (total * (1.0 / 32.0)).astype(BF16)

    aside = {
        1: [students_start],
        2: [teacher_duals],
        4: [students_across],
        6: [students_swap],
        8: [student_norms],
        10: [student_swap, student_own],
        12: [student_back],
        14: [lambda: student_out(OUT_THEN)],
        16: [lambda: student_out(OUT_LATER)],
        18: [projection_gradient],
    }
    chains = [chain(0), chain(1)]
    for stage in range(20):
        for one in chains:
            next(one)
        for work in aside.get(stage, []):
            work()

    arrive(state["back"])
    state["keep"].wait()
    for copy in sent:
        copy.wait_send()


def deliver(gp_in, gs_in, gst_in, gp_ref, gs_ref, gst_ref, gp, gs, gst, sem):
    moves = [(gp_in, gp, gp_ref), (gs_in, gs, gs_ref)]
    part = gst_in.shape[0] // 4
    for i in range(4):
        rows = pl.ds(i * part, part)
        moves.append((gst_in.at[rows], gst.at[rows], gst_ref.at[rows]))
    loads = [pltpu.make_async_copy(a, b, sem.at[0, i]) for i, (a, b, _) in enumerate(moves)]
    stores = [pltpu.make_async_copy(b, c, sem.at[1, i]) for i, (_, b, c) in enumerate(moves)]
    for load in loads:
        load.start()
    for load, store in zip(loads, stores):
        load.wait()
        store.start()
    for store in stores:
        store.wait()


def per_device(
    teacher_ids, slab_embed, projection, learner_vector_table, teacher_dual, student_dual
):
    ids = teacher_ids.reshape(2, 1, ROWS // 2)
    duals = teacher_dual.reshape(teacher_dual.shape[0] // 128, 128)
    sdual = student_dual.reshape(8, 1, 256)
    vmem = pl.BlockSpec(memory_space=pltpu.VMEM)
    bf, ff = (lambda *n: pltpu.VMEM(n, BF16)), (lambda *n: pltpu.VMEM(n, F32))
    anywhere = pl.BlockSpec(memory_space=pl.ANY)
    shapes = (
        jax.ShapeDtypeStruct(projection.shape, BF16),
        jax.ShapeDtypeStruct(slab_embed.shape, BF16),
        jax.ShapeDtypeStruct(learner_vector_table.shape, BF16),
    )
    results = pl.pallas_call(
        kernel,
        out_shape=shapes,
        in_specs=[vmem, vmem, anywhere, anywhere, anywhere, vmem],
        out_specs=(vmem, vmem, anywhere),
        scratch_shapes=[
            pltpu.VMEM(projection.shape, BF16),
            pltpu.VMEM(duals.shape, F32),
            bf(8, 128, 256),
            bf(2, 256, DS),
            ff(1, 256),
            ff(2, 4, 64, FB),
            ff(2, 4, 64, FB),
            ff(2, 4, 64, FB),
            bf(2, 4, 64, FB),
            bf(2, 3, 64, FB),
            bf(2, 64, FB),
            bf(2, 3, 16, FB),
            bf(2, 16, FB),
            bf(2, 2, 4, 4, 64, FB),
            ff(16, 128),
            ff(2, 4, 64, 128),
            ff(2, 1, 256),
            bf(2, 128, 256),
            bf(2, 2, 256, 256),
            bf(2, 2, 4, 4, 64, FB),
            bf(2, 2, 2, 2, 4, 16, FB),
            bf(2, 2, 2, 2, 2, 4, 16, FB),
            bf(2, 2, 4, 64, FB),
            bf(2, 3, 2, 64, FB),
            bf(2, 2, 64, FB),
            bf(2, 7, 16, FB),
            bf(2, 16, FB),
            bf(2, 2, 4, 64, FB),
            bf(256, DS),
            bf(256, DS),
            ff(256, DS),
            bf(256, DS),
            bf(2, 7, 64, 256),
            bf(2, 7, 64, 256),
            pltpu.SemaphoreType.DMA((NSEM,)),
            pltpu.SemaphoreType.DMA((NSEM,)),
            pltpu.SemaphoreType.DMA((4,)),
        ],
        compiler_params=pltpu.CompilerParams(
            collective_id=0, has_side_effects=True, vmem_limit_bytes=56 * 1024 * 1024
        ),
        cost_estimate=pl.CostEstimate(flops=5_500_000_000, bytes_accessed=5_000_000, transcendentals=262144),
    )(ids, slab_embed, projection, learner_vector_table, duals, sdual)
    return pl.pallas_call(
        deliver,
        out_shape=shapes,
        in_specs=[anywhere] * 3,
        out_specs=(anywhere,) * 3,
        scratch_shapes=[pltpu.VMEM(shape.shape, BF16) for shape in shapes] + [pltpu.SemaphoreType.DMA((2, 6))],
        compiler_params=pltpu.CompilerParams(vmem_limit_bytes=60 * 1024 * 1024),
    )(*results)


def solution(mesh):
    in_specs = (P(), P("slab", "vocab"), P("vocab", "slab"), P("vocab", "slab"), P(), P("vocab"))
    out_specs = (P("vocab", "slab"), P("slab", "vocab"), P("vocab", "slab"))
    return jax.shard_map(
        per_device, mesh=mesh, in_specs=in_specs, out_specs=out_specs, check_vma=False
    )
```

```python
import jax
import jax.numpy as jnp
from jax import lax
from jax.experimental import pallas as pl
from jax.experimental.pallas import tpu as pltpu
from jax.sharding import PartitionSpec as P

DS = 3072
ROWS = 1024
VOCAB = 65536
STRENGTH = 0.04
FB = 384
NSEM = 224
IN_FIRST, IN_LATER = ((1, 1), (3, 1), (1, 0), (3, 0), (2, 0)), ((2, 1), (0, 1))
OUT_FIRST, OUT_THEN, OUT_LATER = ((1, 1), (3, 1)), ((1, 0), (3, 0), (2, 0)), ((2, 1), (0, 1))
F32, BF16 = jnp.float32, jnp.bfloat16
MESH = pl.DeviceIdType.MESH


def dot_last(a, b):
    return lax.dot_general(a, b, (((1,), (1,)), ((), ())), preferred_element_type=F32)


def dot_first(a, b):
    return lax.dot_general(a, b, (((0,), (0,)), ((), ())), preferred_element_type=F32)


def dot(a, b):
    return jnp.dot(a, b, preferred_element_type=F32)


def al(value, size):
    return pl.multiple_of(value, size)


def kernel(
    ids_ref, slab_ref, proj_hbm, table_ref, dual_hbm, sdual_ref,
    gp_ref, gs_ref, gst_ref,
    proj_ref, dual_ref, xg, sx, sdb, crecv, csend, acc, xsend, xrecv, zsend, zrecv, pown, pbuf,
    dtail, rd, qrow, kb, kt, rbuf, rfirst, rlast, rmid, rgot, rz, rzr,
    rgown, rg, stsend, strecv, stown, gown, fsend, frecv,
    ssem, rsem, lsem,
):
    s = lax.axis_index("slab")
    v = lax.axis_index("vocab")
    zlo, y = lax.div(s, 4), lax.rem(s, 4)
    core, zhi, x = lax.rem(v, 2), lax.rem(lax.div(v, 2), 4), lax.div(v, 8)
    other, zother = 1 - core, 1 - zlo

    def at_slab(d):
        return (lax.rem(s + d, 8), v)

    def at_x(d):
        return (s, lax.rem(x + d, 4) * 8 + zhi * 2 + core)

    def at_y(d):
        return (zlo * 4 + lax.rem(y + d, 4), v)

    def at_yz(d, b):
        return (lax.rem(zlo + b, 2) * 4 + lax.rem(y + d, 4), v)

    def at_z(a, b):
        return (lax.rem(zlo + b, 2) * 4 + y, x * 8 + lax.rem(zhi + a, 4) * 2 + core)

    sibling = (s, x * 8 + zhi * 2 + other)
    slab_order = [(2, 1), (1, 1), (3, 1), (2, 0), (1, 0), (3, 0), (0, 1)]
    z_peers = [(a, b) for a in (2, 1, 3, 0) for b in range(2) if a or b]

    used = [0]
    sent = []

    def send(src, dst, device):
        i = used[0]
        used[0] += 1
        copy = pltpu.make_async_remote_copy(
            src_ref=src, dst_ref=dst, send_sem=ssem.at[i], recv_sem=rsem.at[i],
            device_id=device, device_id_type=MESH,
        )
        copy.start()
        return copy

    def arrive(copies):
        for copy in copies:
            copy.wait_recv()
        sent.extend(copies)

    class Gather:
        def __init__(self, view, index, at):
            self.view, self.index, self.at = view, index, at
            a, b = view(index, 0), view(index, 1)
            self.first = [send(a, a, at(1)), send(b, b, at(3))]
            self.rest = [send(b, b, at(1)), send(a, a, at(3))]

        def forward(self):
            arrive(self.first[:1])
            block = self.view(lax.rem(self.index + 3, 4), 0)
            self.rest.append(send(block, block, self.at(1)))
            arrive(self.first[1:])
            block = self.view(lax.rem(self.index + 1, 4), 1)
            self.rest.append(send(block, block, self.at(3)))

        def finish(self):
            arrive(self.rest)

    class Reduce:
        def __init__(self, view, index, at, first, last, own=None):
            self.view, self.index, self.at, self.first, self.last = view, index, at, first, last
            self.own = own or (lambda j, h: view(j, h)[...].astype(F32))
            right, left, far = [lax.rem(index + d, 4) for d in (1, 3, 2)]
            self.right, self.left = right, left
            self.head = [send(view(far, 0), first.at[0], at(1)), send(view(far, 1), first.at[1], at(3))]
            self.rest = [send(view(right, 1), last.at[0, 1], at(1)), send(view(left, 0), last.at[1, 0], at(3))]

        def forward(self):
            arrive(self.head[:1])
            block = self.view(self.right, 0)
            block[...] = (self.own(self.right, 0) + self.first[0].astype(F32)).astype(BF16)
            self.rest.append(send(block, self.last.at[0, 0], self.at(1)))
            arrive(self.head[1:])
            block = self.view(self.left, 1)
            block[...] = (self.own(self.left, 1) + self.first[1].astype(F32)).astype(BF16)
            self.rest.append(send(block, self.last.at[1, 1], self.at(3)))

        def finish(self):
            arrive(self.rest)

        def total(self, h):
            total = self.own(self.index, h) + self.last[0, h].astype(F32)
            return total + self.last[1, h].astype(F32)

    class Spread:
        def __init__(self, block, at):
            self.copies = [send(block, block, at(d)) for d in (2, 1, 3)]

        def finish(self):
            arrive(self.copies)

    class Collect:
        def __init__(self, view, index, at, got):
            self.got = got
            self.copies = [send(view(lax.rem(index + d, 4)), got.at[d - 1], at(d)) for d in (2, 1, 3)]

        def total(self, own):
            arrive(self.copies)
            for d in range(3):
                own += self.got[d].astype(F32)
            return own

    greet = [at_slab(d) for d in range(1, 8)] + [sibling] + [at_x(d) for d in (1, 2, 3)]
    greet += [at_z(a, b) for a, b in z_peers if a]
    barrier = pltpu.get_barrier_semaphore()
    for device in greet:
        pl.semaphore_signal(barrier, inc=1, device_id=device, device_id_type=MESH)
    pl.semaphore_wait(barrier, len(greet))

    mine = al(s * FB, FB)
    own_rows = pl.ds(al(zhi * 16, 16), 16)

    def yz(d, b):
        return lax.rem(zlo + b, 2) * 4 + lax.rem(y + d, 4)

    state = {}
    load_proj = pltpu.make_async_copy(proj_hbm, proj_ref, lsem.at[2])
    load_dual = pltpu.make_async_copy(dual_hbm, dual_ref, lsem.at[3])
    load_proj.start()
    load_dual.start()

    def rows_of(ref, k, c, u):
        rows = slice(u * 32, u * 32 + 32)
        pair = [ref[k, i // 4, i % 4, :, rows, :].reshape(128, FB) for i in (2 * c, 2 * c + 1)]
        return jnp.concatenate(pair, axis=1)

    def affinity(k, u):
        norm = jnp.zeros((128, 1), F32)
        for c in range(4):
            part = rows_of(pbuf, k, c, u).astype(F32)
            norm += jnp.sum(part * part, axis=1, keepdims=True)
        bias = rd[k, :, u * 32 : u * 32 + 32, 0:1].reshape(128, 1)
        bias = (bias - norm * (1.0 / DS)) * (1.0 / STRENGTH)
        mass = jnp.zeros((128, 1), F32)
        for j in range(2):
            inner = jnp.zeros((128, 256), F32)
            for c in range(4):
                inner += dot_last(rows_of(pbuf, k, c, u), sx[j, :, c * 2 * FB : (c + 1) * 2 * FB])
            entry = jnp.exp(bias + qrow[j] + inner * (2.0 / (DS * STRENGTH))).astype(BF16)
            kb[j] = entry
            wide = entry.astype(F32)
            kt[k, j, :, u * 128 : u * 128 + 128] = wide.T.astype(BF16)
            mass += jnp.sum(wide, axis=1, keepdims=True)
        for c in range(4):
            cols = slice(c * 2 * FB, (c + 1) * 2 * FB)
            term = mass * rows_of(pbuf, k, c, u).astype(F32)
            term -= dot(kb[0], sx[0, :, cols])
            term -= dot(kb[1], sx[1, :, cols])
            for i in range(2):
                part = term[:, i * FB : (i + 1) * FB].astype(BF16).reshape(4, 32, FB)
                rbuf[k, (2 * c + i) // 4, (2 * c + i) % 4, :, u * 32 : u * 32 + 32, :] = part

    def slab_term(k, index):
        return dot_last(rg[lax.div(index, 4), k, lax.rem(index, 4)], proj_ref[...])

    def chain(k):
        index_mid, at_mid, index_last, at_last = (x, at_x, y, at_y) if k == 0 else (y, at_y, x, at_x)

        def block_of(ref, u):
            def view(j, h):
                rows = slice(u * 32 + h * 16, u * 32 + h * 16 + 16)
                return ref.at[0, :, j, :, rows, :] if k == 0 else ref.at[1, :, :, j, rows, :]

            return view

        whole = slice(k * 64, k * 64 + 64)
        copies = [send(slab_ref.at[whole, :], xg.at[s, whole, :], at_yz(d, b)) for d, b in slab_order]
        xg[s, whole, :] = slab_ref[whole, :]
        yield
        arrive(copies)
        if k == 0:
            load_proj.wait()
        for i in range(4):
            csend[k, i] = dot(xg[other * 4 + i, whole, :], proj_ref[...])
        pair = send(csend.at[k], crecv.at[k], sibling)
        for i in range(4):
            acc[k, i] = dot(xg[core * 4 + i, whole, :], proj_ref[...])
        yield
        arrive([pair])
        acc[k] = acc[k] + crecv[k]
        xsend[k] = acc[k].astype(BF16)
        collect = Collect(lambda j: xsend.at[k, j], x, at_x, xrecv.at[k])
        yield
        zsend[k] = collect.total(acc[k, x]).astype(BF16)
        copies = []
        for a in (2, 1, 3):
            rows = al(lax.rem(zhi + a, 4) * 16, 16)
            copies.append(send(zsend.at[k, pl.ds(rows, 16), :], zrecv.at[k, a - 1], at_z(a, 0)))
        yield
        arrive(copies)
        total = zsend[k, own_rows, :].astype(F32)
        for a in range(3):
            total += zrecv[k, a].astype(F32)
        pown[k] = total.astype(BF16)
        place = pbuf.at[k, zlo, y, x, own_rows, :]
        copies = [send(pown.at[k], place, at_z(a, b)) for a, b in z_peers]
        pbuf[k, zlo, y, x, own_rows, :] = pown[k]
        yield
        arrive(copies)
        spread = Spread(pbuf.at[k, :, y, x], at_mid)
        yield
        spread.finish()
        gathers = [Gather(block_of(pbuf, u), index_last, at_last) for u in range(2)]
        yield
        gathers[0].forward()
        yield
        gathers[1].forward()
        yield
        reduces = []
        for u in range(2):
            gathers[u].finish()
            affinity(k, u)
            reduces.append(Reduce(block_of(rbuf, u), index_last, at_last, rfirst.at[k, u], rlast.at[k, u]))
            yield
        reduces[0].forward()
        yield
        reduces[1].forward()
        yield
        for u in range(2):
            reduces[u].finish()
            for h in range(2):
                rmid[k, :, :, u * 32 + h * 16 : u * 32 + h * 16 + 16, :] = reduces[u].total(h).astype(BF16)
        collect = Collect(lambda j: rmid.at[k, :, j], index_mid, at_mid, rgot.at[k])
        yield
        rz[k] = collect.total(rmid[k, :, index_mid].astype(F32)).astype(BF16)
        copies = []
        for i, (a, b) in enumerate(z_peers):
            rows = al(lax.rem(zhi + a, 4) * 16, 16)
            copies.append(send(rz.at[k, lax.rem(zlo + b, 2), pl.ds(rows, 16), :], rzr.at[k, i], at_z(a, b)))
        yield
        arrive(copies)
        total = rz[k, zlo, own_rows, :].astype(F32)
        for i in range(7):
            total += rzr[k, i].astype(F32)
        rgown[k] = (total * (1.0 / VOCAB)).astype(BF16)
        copies = [send(rgown.at[k], rg.at[core, k, x, own_rows, :], at_z(a, 0)) for a in (2, 1, 3)]
        rg[core, k, x, own_rows, :] = rgown[k]
        yield
        arrive(copies)
        spread = Spread(rg.at[core, k, x], at_x)
        yield
        spread.finish()
        pair = send(rg.at[core, k], rg.at[core, k], sibling)
        yield
        arrive([pair])
        copies = []
        for i, (d, b) in enumerate(slab_order):
            fsend[k, i] = slab_term(k, yz(d, b)).astype(BF16)
            copies.append(send(fsend.at[k, i], frecv.at[k, i], at_yz(d, b)))
        yield
        total = slab_term(k, s)
        arrive(copies)
        for i in range(7):
            total += frecv[k, i].astype(F32)
        gs_ref[whole, :] = total.astype(BF16)
        yield

    def student_block(d, b):
        rows = al(yz(d, b) * 256, 256)
        return send(table_ref.at[pl.ds(rows, 256), :], sx.at[0, :, pl.ds(mine, FB)], at_yz(d, b))

    def students_start():
        state["students"] = [student_block(d, b) for d, b in IN_FIRST]
        state["local"] = pltpu.make_async_copy(
            table_ref.at[pl.ds(al(s * 256, 256), 256), :], sx.at[0, :, pl.ds(mine, FB)], lsem.at[0]
        )
        state["local"].start()
        state["duals"] = send(sdual_ref.at[s], sdb, sibling)

    def students_across():
        state["students"] += [student_block(d, b) for d, b in IN_LATER]

    def students_swap():
        arrive(state["students"])
        state["local"].wait()
        state["both"] = send(sx.at[0], sx.at[1], sibling)

    def teacher_duals():
        ids = ids_ref[core]
        high, low = lax.div(ids, 128), lax.rem(ids, 128)
        found = jnp.zeros((128, 512), F32)
        load_dual.wait()
        dtail[...] = jnp.zeros_like(dtail)
        whole = dual_ref.shape[0] // 16 * 16
        dtail[0 : dual_ref.shape[0] - whole, :] = dual_ref[whole:, :]
        half = whole // 2
        for base, rest in ((0, dual_ref[0:half, :]), (half, dual_ref[half:whole, :]), (whole, dtail[...])):
            hot = lax.broadcasted_iota(jnp.int32, (rest.shape[0], 512), 0) + base == high
            hot = hot.astype(F32).astype(BF16)
            for _ in range(3):
                part = rest.astype(BF16)
                found += dot_first(part, hot)
                rest = rest - part.astype(F32)
        lane = lax.broadcasted_iota(jnp.int32, (128, 512), 0) == low
        row = jnp.sum(jnp.where(lane, found, 0.0), axis=0, keepdims=True)
        column = jnp.broadcast_to(row, (128, 512)).T
        for k in range(2):
            for i in range(4):
                rd[k, i] = column[i * 128 + k * 64 : i * 128 + k * 64 + 64]

    def student_norms():
        arrive([state["both"], state["duals"]])
        for j in range(2):
            norm = jnp.zeros((256, 1), F32)
            for c in range(8):
                part = sx[j, :, c * FB : (c + 1) * FB].astype(F32)
                norm += jnp.sum(part * part, axis=1, keepdims=True)
            norm = jnp.broadcast_to(norm, (256, 128)).T[0:1]
            dual = sdual_ref[s] if j == 0 else sdb[...]
            qrow[j] = (dual - norm * (1.0 / DS)) * (1.0 / STRENGTH)

    def student_term(j, c, mass):
        cols = slice(c * 2 * FB, (c + 1) * 2 * FB)
        term = mass * sx[j, :, cols].astype(F32)
        for k in range(2):
            rows = jnp.concatenate([rows_of(pbuf, k, c, u) for u in range(2)], axis=0)
            term -= dot(kt[k, j], rows)
        return cols, term

    def student_mass(j):
        wide = kt[0, j].astype(F32) + kt[1, j].astype(F32)
        return jnp.sum(wide, axis=1, keepdims=True)

    def student_swap():
        mass = student_mass(1)

        for c in range(4):
            cols, term = student_term(1, c, mass)
            stsend[:, cols] = term.astype(BF16)

        state["swap"] = send(stsend, strecv, sibling)

    def student_own():
        mass = student_mass(0)

        for c in range(4):
            cols, term = student_term(0, c, mass)
            stown[:, cols] = term

    srows = al(s * 256, 256)

    def student_out(places):
        for d, b in places:
            cols = pl.ds(al(yz(d, b) * FB, FB), FB)
            state["back"].append(
                send(gown.at[:, cols], gst_ref.at[pl.ds(srows, 256), :], at_yz(d, b))
            )

    def student_back():
        arrive([state["swap"]])

        @pl.loop(0, 8)
        def _(c):
            cols = pl.ds(al(c * FB, FB), FB)
            gown[:, cols] = ((stown[:, cols] + strecv[:, cols].astype(F32)) * (1.0 / ROWS)).astype(BF16)

        state["back"] = []
        student_out(OUT_FIRST)
        state["keep"] = pltpu.make_async_copy(
            gown.at[:, pl.ds(mine, FB)], gst_ref.at[pl.ds(srows, 256), :], lsem.at[1]
        )
        state["keep"].start()

    def projection_gradient():
        total = jnp.zeros((256, FB), F32)
        for i in range(8):
            grad = jnp.concatenate([rg[i // 4, 0, i % 4], rg[i // 4, 1, i % 4]], axis=0)
            total += dot_first(xg[i], grad)
        gp_ref[...] = (total * (1.0 / 32.0)).astype(BF16)

    aside = {
        1: [students_start],
        2: [teacher_duals],
        4: [students_across],
        6: [students_swap],
        8: [student_norms],
        10: [student_swap, student_own],
        12: [student_back],
        14: [lambda: student_out(OUT_THEN)],
        16: [lambda: student_out(OUT_LATER)],
        18: [projection_gradient],
    }
    chains = [chain(0), chain(1)]
    for stage in range(20):
        for one in chains:
            next(one)
        for work in aside.get(stage, []):
            work()

    arrive(state["back"])
    state["keep"].wait()
    for copy in sent:
        copy.wait_send()


def deliver(gp_in, gs_in, gst_in, gp_ref, gs_ref, gst_ref, gp, gs, gst, sem):
    moves = [(gp_in, gp, gp_ref), (gs_in, gs, gs_ref)]
    part = gst_in.shape[0] // 4
    for i in range(4):
        rows = pl.ds(i * part, part)
        moves.append((gst_in.at[rows], gst.at[rows], gst_ref.at[rows]))
    loads = [pltpu.make_async_copy(a, b, sem.at[0, i]) for i, (a, b, _) in enumerate(moves)]
    stores = [pltpu.make_async_copy(b, c, sem.at[1, i]) for i, (_, b, c) in enumerate(moves)]
    for load in loads:
        load.start()
    for load, store in zip(loads, stores):
        load.wait()
        store.start()
    for store in stores:
        store.wait()


def per_device(
    teacher_ids, slab_embed, projection, learner_vector_table, teacher_dual, student_dual
):
    ids = teacher_ids.reshape(2, 1, ROWS // 2)
    duals = teacher_dual.reshape(teacher_dual.shape[0] // 128, 128)
    sdual = student_dual.reshape(8, 1, 256)
    vmem = pl.BlockSpec(memory_space=pltpu.VMEM)
    bf, ff = (lambda *n: pltpu.VMEM(n, BF16)), (lambda *n: pltpu.VMEM(n, F32))
    anywhere = pl.BlockSpec(memory_space=pl.ANY)
    shapes = (
        jax.ShapeDtypeStruct(projection.shape, BF16),
        jax.ShapeDtypeStruct(slab_embed.shape, BF16),
        jax.ShapeDtypeStruct(learner_vector_table.shape, BF16),
    )
    results = pl.pallas_call(
        kernel,
        out_shape=shapes,
        in_specs=[vmem, vmem, anywhere, anywhere, anywhere, vmem],
        out_specs=(vmem, vmem, anywhere),
        scratch_shapes=[
            pltpu.VMEM(projection.shape, BF16),
            pltpu.VMEM(duals.shape, F32),
            bf(8, 128, 256),
            bf(2, 256, DS),
            ff(1, 256),
            ff(2, 4, 64, FB),
            ff(2, 4, 64, FB),
            ff(2, 4, 64, FB),
            bf(2, 4, 64, FB),
            bf(2, 3, 64, FB),
            bf(2, 64, FB),
            bf(2, 3, 16, FB),
            bf(2, 16, FB),
            bf(2, 2, 4, 4, 64, FB),
            ff(16, 128),
            ff(2, 4, 64, 128),
            ff(2, 1, 256),
            bf(2, 128, 256),
            bf(2, 2, 256, 256),
            bf(2, 2, 4, 4, 64, FB),
            bf(2, 2, 2, 2, 4, 16, FB),
            bf(2, 2, 2, 2, 2, 4, 16, FB),
            bf(2, 2, 4, 64, FB),
            bf(2, 3, 2, 64, FB),
            bf(2, 2, 64, FB),
            bf(2, 7, 16, FB),
            bf(2, 16, FB),
            bf(2, 2, 4, 64, FB),
            bf(256, DS),
            bf(256, DS),
            ff(256, DS),
            bf(256, DS),
            bf(2, 7, 64, 256),
            bf(2, 7, 64, 256),
            pltpu.SemaphoreType.DMA((NSEM,)),
            pltpu.SemaphoreType.DMA((NSEM,)),
            pltpu.SemaphoreType.DMA((4,)),
        ],
        compiler_params=pltpu.CompilerParams(
            collective_id=0, has_side_effects=True, vmem_limit_bytes=56 * 1024 * 1024
        ),
        cost_estimate=pl.CostEstimate(flops=5_500_000_000, bytes_accessed=5_000_000, transcendentals=262144),
    )(ids, slab_embed, projection, learner_vector_table, duals, sdual)
    return pl.pallas_call(
        deliver,
        out_shape=shapes,
        in_specs=[anywhere] * 3,
        out_specs=(anywhere,) * 3,
        scratch_shapes=[pltpu.VMEM(shape.shape, BF16) for shape in shapes] + [pltpu.SemaphoreType.DMA((2, 6))],
        compiler_params=pltpu.CompilerParams(vmem_limit_bytes=60 * 1024 * 1024),
    )(*results)


def solution(mesh):
    in_specs = (P(), P("slab", "vocab"), P("vocab", "slab"), P("vocab", "slab"), P(), P("vocab"))
    out_specs = (P("vocab", "slab"), P("slab", "vocab"), P("vocab", "slab"))
    return jax.shard_map(
        per_device, mesh=mesh, in_specs=in_specs, out_specs=out_specs, check_vma=False
    )
```
